32 devices in a mesh: group: 2 (over y), dp: 4 (over x, core), tensor: 4 (over z).
Axes of the slice: x: 2, y: 2, z: 4, core: 2. Of those that a mesh axis runs over, the one named last changes fastest.
Arguments:
- tokens: bfloat16 [8192, 1024], P(('group', 'dp')), parts along dimension 0, may hold values from -6 to 6
- past_states: float32 [256, 8, 128, 128], P(('group', 'dp'), 'tensor'), parts along dimension 0, may hold values from -3 to 3
- attn_weights: bfloat16 [5, 1024, 1024], P(None, 'dp', 'tensor'), may hold values from -0.1875 to 0.1875
- ffn_weights: bfloat16 [2, 1024, 4096], P(None, 'dp', 'tensor'), may hold values from -0.1875 to 0.1875
- norm_gains: float32 [2, 1024], replicated, may hold values from 0.1 to 1.9
- head_rates: float32 [8], replicated, may hold values from 0.004 to 0.15
- end_lengths: int32 [256], P(('group', 'dp')), parts along dimension 0, may hold values from 1 to 64, as said below
- new_slot: int32 [256], P(('group', 'dp')), parts along dimension 0, may hold values from 0 to 127, as said below
Outputs:
- next_tokens: bfloat16 [8192, 1024], P(('group', 'dp'), 'tensor'), parts along dimension 0
- moved_states: float32 [256, 8, 128, 128], P(('group', 'dp'), 'tensor'), parts along dimension 0
The draws below stay inside these ranges and needn't reach their ends.
There are 2 independent parts, one for each index of `group`. The reference program is written for one: setup_inputs(seed, part) draws one part's arguments, and reference() takes and returns one part's arrays. A program takes and returns all parts, laid end to end along the dimension named above; an argument that names none is the same for every part. Nothing has to cross between parts.
Inputs may be any that keep to these rules, and one draw needn't show every extreme that they name: `end_lengths`: of the sessions in one aligned block of 32 sessions whose end lengths exceed 32, at most 16 have new slots in one aligned block of 32 slots, and some pair of blocks has exactly 16. `new_slot`: A permutation of the 128 slots.
All inputs are finite; a program needn't handle non-finite values.
Results may differ from the reference program's by a relative error of at most 0.018.
Values may be sent and summed in bfloat16 or wider, within the bound.
A program may use at most 64 MiB of HBM per device.

```python
import math
import jax
import jax.numpy as jnp
from jax import lax

D = 1024
HEADS = 8
HD = 128
FF = 4096
EVENTS = 32
SESS_DEV = 32
SESSIONS = 128
TOKENS = 4096
PAIR = 16
N_TENSOR = 4


def joint_draw(key):
    base = jax.random.fold_in(key, 4242)
    subkeys = jax.random.split(base, 6)
    blocks = SESSIONS // SESS_DEV
    groups = SESSIONS // PAIR
    inner = jax.vmap(lambda subkey: jax.random.permutation(subkey, SESS_DEV))(jax.random.split(subkeys[0], blocks))
    session_order = (jnp.arange(blocks, dtype=jnp.int32)[:, None] * SESS_DEV + inner.astype(jnp.int32)).reshape(-1)
    group_dest = jax.random.permutation(subkeys[1], groups).astype(jnp.int32)
    position = jnp.arange(SESSIONS, dtype=jnp.int32)
    slot_at = group_dest[position // PAIR] * PAIR + position % PAIR
    new_slot = jnp.zeros((SESSIONS,), jnp.int32).at[session_order].set(slot_at)
    block_of = position // SESS_DEV
    level = jax.random.randint(subkeys[2], (blocks,), 2, 5)
    candidate = jax.random.randint(subkeys[3], (SESSIONS,), 0, 4) < level[block_of]
    chosen = jax.random.randint(subkeys[4], (), 0, groups)
    forced = jnp.zeros((SESSIONS,), bool).at[session_order].set(position // PAIR == chosen)
    candidate = candidate | forced
    pair_id = block_of * blocks + new_slot // SESS_DEV
    ahead = forced[None, :] & ~forced[:, None] | (forced[None, :] == forced[:, None]) & (position[None, :] < position[:, None])
    pair_rank = jnp.sum(candidate[None, :] & (pair_id[None, :] == pair_id[:, None]) & ahead, axis=1)
    survive = candidate & (pair_rank < PAIR)
    long_len = jax.random.randint(subkeys[5], (SESSIONS,), EVENTS + 1, 2 * EVENTS + 1)
    short_len = jax.random.randint(jax.random.fold_in(subkeys[5], 1), (SESSIONS,), 1, EVENTS + 1)
    lengths = jnp.where(survive, long_len, short_len).astype(jnp.int32)
    return (lengths, new_slot)


def draw_end_lengths(key, part):
    return joint_draw(key)[0]


def draw_new_slot(key, part):
    return joint_draw(key)[1]


def block_levels(stream_key, extent, shards, smallest, high):
    loudness = 1.0
    for axis_at, blocks in shards:
        steps = jax.random.uniform(jax.random.fold_in(jax.random.fold_in(stream_key, 6), axis_at), (blocks,), jnp.float32, smallest / len(shards), high / len(shards))
        loudness = loudness * jnp.repeat(jnp.exp(steps), extent[axis_at] // blocks).reshape((-1,) + (1,) * (len(extent) - 1 - axis_at))
    return loudness


def normal_values(key, shape, width, limit, shards=(), kind=jnp.bfloat16):
    factor_of = block_levels(key, shape, shards, -0.22, 0.18) if shards else 1.0
    entries = jax.random.normal(key, shape, jnp.float32) * width * factor_of
    return jnp.minimum(jnp.maximum(entries, -limit), limit).astype(kind)


def setup_inputs(seed: int = 0, part: int = 0) -> dict:
    arg_keys = jax.random.split(jax.random.key(seed), 9)
    part_splits = jax.random.split(jax.random.fold_in(arg_keys[8], part), 9)
    return {
        "tokens": normal_values(part_splits[0], (TOKENS, D), 1.0, 6.0, ((0, 4),)),
        "past_states": normal_values(part_splits[1], (SESSIONS, HEADS, HD, HD), 0.3, 3.0, ((0, 4), (1, 4)), jnp.float32),
        "attn_weights": normal_values(arg_keys[2], (5, D, HEADS * HD), D ** -0.5, 0.1875, ((1, 4), (2, 4))),
        "ffn_weights": normal_values(arg_keys[3], (2, D, FF), D ** -0.5, 0.1875, ((1, 4), (2, 4))),
        "norm_gains": jnp.clip(1.0 + 0.18 * jax.random.normal(arg_keys[4], (2, D), jnp.float32), 0.1, 1.9),
        "head_rates": jnp.clip(jnp.exp(jax.random.uniform(arg_keys[5], (HEADS,), jnp.float32, math.log(0.004), math.log(0.15))), 0.004, 0.15),
        "end_lengths": draw_end_lengths(jax.random.fold_in(jax.random.fold_in(arg_keys[8], part), 71), part),
        "new_slot": draw_new_slot(jax.random.fold_in(jax.random.fold_in(arg_keys[8], part), 71), part),
    }


def rms_scale(values, gain_row):
    meansq = lax.optimization_barrier(jnp.mean(values * values, axis=-1, keepdims=True))
    return (values * lax.rsqrt(meansq + 1e-05) * gain_row).astype(jnp.bfloat16)

def update_state(past_block, key_rows, value_rows, head_decay):
    event_count = key_rows.shape[2]
    position = jnp.arange(event_count).astype(jnp.float32)
    key_scale = key_rows.shape[3] ** (-0.5)
    factor = jnp.exp(-head_decay[:, None] * (event_count - 1.0 - position)[None, :])
    weighted = key_rows.astype(jnp.float32) * key_scale * factor[:, :, None]
    carried = jnp.exp(-head_decay * event_count)[:, None, None] * past_block
    return carried + jnp.einsum('ghjd,ghje->ghde', weighted, value_rows.astype(jnp.float32), precision=lax.Precision.HIGHEST)

def retain_events(query, key_rows, value_rows, past_block, head_decay):
    event_count = query.shape[2]
    position = jnp.arange(event_count).astype(jnp.float32)
    distance = position[:, None] - position[None, :]
    decay = jnp.where(distance >= 0, jnp.exp(-head_decay[:, None, None] * jnp.maximum(distance, 0.0)), 0.0)
    key_scale = query.shape[3] ** (-0.5)
    scores = jnp.einsum('ghid,ghjd->ghij', query.astype(jnp.float32), key_rows.astype(jnp.float32)) * key_scale
    weights_mix = (scores * decay).astype(jnp.bfloat16)
    intra_term = jnp.einsum('ghij,ghje->ghie', weights_mix.astype(jnp.float32), value_rows.astype(jnp.float32))
    inter_factor = jnp.exp(-head_decay[:, None] * (position[None, :] + 1.0))[:, :, None]
    inter_term = jnp.einsum('ghid,ghde->ghie', query.astype(jnp.float32), past_block, precision=lax.Precision.HIGHEST) * inter_factor
    return intra_term + inter_term

def round_trip(values):
    return lax.optimization_barrier(values.astype(jnp.bfloat16)).astype(jnp.float32)

def reference(tokens, past_states, attn_weights, ffn_weights, norm_gains, head_rates, end_lengths, new_slot):
    live_len = jnp.minimum(end_lengths, EVENTS)
    survive = end_lengths > EVENTS
    float_tokens = tokens.astype(jnp.float32)
    normed = rms_scale(float_tokens, norm_gains[0])
    projected = [jnp.dot(normed, attn_weights[which], preferred_element_type=jnp.float32) for which in range(4)]

    def split_heads(matrix):
        return matrix.reshape(SESSIONS, EVENTS, HEADS, HD).transpose(0, 2, 1, 3)
    query = split_heads(projected[0].astype(jnp.bfloat16))
    key_rows = split_heads(projected[1].astype(jnp.bfloat16))
    value_rows = split_heads(projected[2].astype(jnp.bfloat16))
    gate_rows = projected[3]
    retained = retain_events(query, key_rows, value_rows, past_states, head_rates)
    new_states = update_state(past_states, key_rows, value_rows, head_rates)
    row_mean = lax.optimization_barrier(jnp.mean(retained, axis=-1, keepdims=True))
    centred = retained - row_mean
    row_var = lax.optimization_barrier(jnp.mean(centred * centred, axis=-1, keepdims=True))
    normalised = centred * lax.rsqrt(row_var + 1e-05)
    merged = normalised.transpose(0, 2, 1, 3).reshape(TOKENS, HEADS * HD)
    gated = (jax.nn.silu(gate_rows) * merged).astype(jnp.bfloat16)
    group_cols = HEADS * HD // N_TENSOR
    attended = jnp.zeros((TOKENS, D), jnp.float32)
    for group_idx in range(N_TENSOR):
        start_col = group_idx * group_cols
        term = jnp.dot(gated[:, start_col:start_col + group_cols], attn_weights[4][:, start_col:start_col + group_cols].T, preferred_element_type=jnp.float32)
        attended = attended + round_trip(term)
    residual = float_tokens + attended
    hidden_in = rms_scale(residual, norm_gains[1])
    activated = jax.nn.gelu(jnp.dot(hidden_in, ffn_weights[0], preferred_element_type=jnp.float32), approximate=True).astype(jnp.bfloat16)
    unit_cols = FF // N_TENSOR
    ffn_out = jnp.zeros((TOKENS, D), jnp.float32)
    for group_idx in range(N_TENSOR):
        start_col = group_idx * unit_cols
        term = jnp.dot(activated[:, start_col:start_col + unit_cols], ffn_weights[1][:, start_col:start_col + unit_cols].T, preferred_element_type=jnp.float32)
        ffn_out = ffn_out + round_trip(term)
    keep_rows = (jnp.arange(EVENTS, dtype=jnp.int32)[None, :] < live_len[:, None]).reshape(-1)
    next_tokens = jnp.where(keep_rows[:, None], residual + ffn_out, 0.0).astype(jnp.bfloat16)
    inverse = jnp.zeros((SESSIONS,), jnp.int32).at[new_slot].set(jnp.arange(SESSIONS, dtype=jnp.int32))
    moved_states = jnp.where(survive[inverse][:, None, None, None], new_states[inverse], 0.0)
    return (next_tokens, moved_states)
```

```python
import jax
import jax.numpy as jnp
from jax import lax
from jax.experimental import pallas as pl
from jax.experimental.pallas import tpu as pltpu
from jax.sharding import PartitionSpec as P


def pick_kernel(index_ref, keep_ref, values_ref, out_ref):
    def body(at, carry):
        kept = keep_ref[at].astype(jnp.float32)
        out_ref[at] = jnp.where(
            kept > 0, values_ref[index_ref[at]].astype(jnp.float32), 0.0
        ).astype(out_ref.dtype)
        return carry

    lax.fori_loop(0, out_ref.shape[0], body, 0)


def pick(values, index, keep, dtype):
    return pl.pallas_call(
        pick_kernel,
        out_shape=jax.ShapeDtypeStruct(index.shape + values.shape[1:], dtype),
        in_specs=[pl.BlockSpec(memory_space=pltpu.SMEM)] * 2
        + [pl.BlockSpec(memory_space=pltpu.VMEM)],
        out_specs=pl.BlockSpec(memory_space=pltpu.VMEM),
        compiler_params=pltpu.CompilerParams(vmem_limit_bytes=48 * 2**20),
    )(index.astype(jnp.int32), keep.astype(jnp.int32), values)


def rms_scale(values, gain_row):
    meansq = jnp.mean(values * values, axis=-1, keepdims=True)
    return (values * lax.rsqrt(meansq + 1e-05) * gain_row).astype(jnp.bfloat16)


def update_state(past_block, key_rows, value_rows, head_decay):
    event_count = key_rows.shape[2]
    position = jnp.arange(event_count).astype(jnp.float32)
    key_scale = key_rows.shape[3] ** (-0.5)
    factor = jnp.exp(-head_decay[:, None] * (event_count - 1.0 - position)[None, :])
    weighted = key_rows.astype(jnp.float32) * key_scale * factor[:, :, None]
    carried = jnp.exp(-head_decay * event_count)[:, None, None] * past_block
    return carried + jnp.einsum(
        "ghjd,ghje->ghde", weighted.astype(jnp.bfloat16), value_rows, preferred_element_type=jnp.float32
    )


def retain_events(query, key_rows, value_rows, past_block, head_decay):
    event_count = query.shape[2]
    position = jnp.arange(event_count).astype(jnp.float32)
    distance = position[:, None] - position[None, :]
    decay = jnp.where(
        distance >= 0, jnp.exp(-head_decay[:, None, None] * jnp.maximum(distance, 0.0)), 0.0
    )
    key_scale = query.shape[3] ** (-0.5)
    scores = (
        jnp.einsum("ghid,ghjd->ghij", query, key_rows, preferred_element_type=jnp.float32)
        * key_scale
    )
    weights_mix = (scores * decay).astype(jnp.bfloat16)
    intra_term = jnp.einsum(
        "ghij,ghje->ghie", weights_mix, value_rows, preferred_element_type=jnp.float32
    )
    inter_factor = jnp.exp(-head_decay[:, None] * (position[None, :] + 1.0))[:, :, None]
    inter_term = (
        jnp.einsum(
            "ghid,ghde->ghie",
            query,
            past_block.astype(jnp.bfloat16),
            preferred_element_type=jnp.float32,
        )
        * inter_factor
    )
    return intra_term + inter_term


def per_device(
    tokens, past_states, attn_weights, ffn_weights, norm_gains, head_rates, end_lengths, new_slot
):
    sessions_here = end_lengths.shape[0]
    row_count = tokens.shape[0]
    event_count = row_count // sessions_here
    heads_here = past_states.shape[1]
    head_dim = past_states.shape[3]
    tensor_at = lax.axis_index("tensor")
    head_decay = lax.dynamic_slice_in_dim(head_rates, tensor_at * heads_here, heads_here)
    peer_count = lax.axis_size("dp")
    pair_cap = max(2, 2 * sessions_here // peer_count)
    slot_count = peer_count * pair_cap
    survive = end_lengths > event_count
    live_len = jnp.minimum(end_lengths, event_count)
    target_dev = new_slot // sessions_here
    local_slot = new_slot % sessions_here
    session_ids = jnp.arange(sessions_here, dtype=jnp.int32)
    earlier = (
        (target_dev[None, :] == target_dev[:, None])
        & survive[None, :]
        & (session_ids[None, :] < session_ids[:, None])
    )
    pair_rank = jnp.sum(earlier, axis=1)
    buffer_pos = target_dev * pair_cap + pair_rank
    matches = (buffer_pos[None, :] == jnp.arange(slot_count, dtype=jnp.int32)[:, None]) & survive[
        None, :
    ]
    source = jnp.sum(jnp.where(matches, session_ids[None, :], 0), axis=1)
    filled = jnp.any(matches, axis=1)
    label_at = jnp.sum(jnp.where(matches, local_slot[None, :], 0), axis=1)
    labels = (
        jnp.where(filled, label_at, -1).astype(jnp.float32).reshape(peer_count, pair_cap)
    )

    sent_labels = lax.all_to_all(
        labels.astype(jnp.bfloat16), "dp", split_axis=0, concat_axis=0, tiled=True
    ).astype(labels.dtype)
    weights_attn = lax.all_gather(attn_weights[:4], "dp", axis=1, tiled=True)
    weights_out = lax.all_gather(attn_weights[4], "dp", axis=0, tiled=True)
    weights_out = lax.all_gather(weights_out, "tensor", axis=1, tiled=True)
    weights_ffn = lax.all_gather(ffn_weights, "dp", axis=1, tiled=True)
    float_tokens = tokens.astype(jnp.float32)
    normed = rms_scale(float_tokens, norm_gains[0])
    projected = jnp.einsum(
        "nd,mde->mne", normed, weights_attn, preferred_element_type=jnp.float32
    )

    def split_heads(matrix):
        return matrix.reshape(sessions_here, event_count, heads_here, head_dim).transpose(
            0, 2, 1, 3
        )

    query = split_heads(projected[0].astype(jnp.bfloat16))
    key_rows = split_heads(projected[1].astype(jnp.bfloat16))
    value_rows = split_heads(projected[2].astype(jnp.bfloat16))
    gate_rows = projected[3]
    retained = retain_events(query, key_rows, value_rows, past_states, head_decay)
    updated = update_state(past_states, key_rows, value_rows, head_decay)
    packed = pick(updated, source, filled, jnp.bfloat16)
    received = lax.all_to_all(
        packed.reshape((peer_count, pair_cap) + packed.shape[1:]), "dp", split_axis=0, concat_axis=0, tiled=True
    )
    flattened = received.reshape((slot_count,) + received.shape[2:])
    found_at = sent_labels.reshape(-1)[None, :] == session_ids[:, None].astype(jnp.float32)
    which_slot = jnp.sum(
        jnp.where(found_at, jnp.arange(slot_count, dtype=jnp.int32)[None, :], 0), axis=1
    )
    present = jnp.any(found_at, axis=1)
    moved_states = pick(flattened, which_slot, present, jnp.float32)
    row_mean = jnp.mean(retained, axis=-1, keepdims=True)
    centred = retained - row_mean
    row_var = jnp.mean(centred * centred, axis=-1, keepdims=True)
    normalised = centred * lax.rsqrt(row_var + 1e-05)
    merged = normalised.transpose(0, 2, 1, 3).reshape(row_count, heads_here * head_dim)
    gated = (jax.nn.silu(gate_rows) * merged).astype(jnp.bfloat16)
    gated_all = lax.all_gather(gated, "tensor", axis=1, tiled=True)
    attended = jnp.einsum("nc,dc->nd", gated_all, weights_out, preferred_element_type=jnp.float32)
    residual = float_tokens + attended
    hidden_in = rms_scale(residual, norm_gains[1])
    activated = jax.nn.gelu(
        jnp.dot(hidden_in, weights_ffn[0], preferred_element_type=jnp.float32), approximate=True
    ).astype(jnp.bfloat16)
    ffn_partial = jnp.einsum(
        "nf,df->nd", activated, weights_ffn[1], preferred_element_type=jnp.float32
    )
    ffn_share = lax.psum_scatter(
        ffn_partial.astype(jnp.bfloat16), "tensor", scatter_dimension=1, tiled=True
    ).astype(jnp.float32)
    col_count = ffn_share.shape[1]
    residual_here = lax.dynamic_slice_in_dim(residual, tensor_at * col_count, col_count, 1)
    keep_rows = (jnp.arange(event_count, dtype=jnp.int32)[None, :] < live_len[:, None]).reshape(-1)
    next_tokens = jnp.where(keep_rows[:, None], residual_here + ffn_share, 0.0).astype(jnp.bfloat16)
    return (next_tokens, moved_states)


def solution(mesh):
    placed = (
        P(("group", "dp"), None),
        P(("group", "dp"), "tensor", None, None),
        P(None, "dp", "tensor"),
        P(None, "dp", "tensor"),
        P(),
        P(),
        P(("group", "dp")),
        P(("group", "dp")),
    )
    return jax.shard_map(
        per_device,
        mesh=mesh,
        in_specs=placed,
        out_specs=(P(("group", "dp"), "tensor"), P(("group", "dp"), "tensor", None, None)),
        check_vma=False,
    )
```

```python
import functools

import jax
import jax.numpy as jnp
from jax import lax
from jax.experimental import pallas as pl
from jax.experimental.pallas import tpu as pltpu
from jax.sharding import PartitionSpec as P


def pick_kernel(index_ref, keep_ref, values_ref, out_ref):
    def body(at, carry):
        kept = keep_ref[at].astype(jnp.float32)
        out_ref[at] = jnp.where(
            kept > 0, values_ref[index_ref[at]].astype(jnp.float32), 0.0
        ).astype(out_ref.dtype)
        return carry

    lax.fori_loop(0, out_ref.shape[0], body, 0)


def pick(values, index, keep, dtype):
    return pl.pallas_call(
        pick_kernel,
        out_shape=jax.ShapeDtypeStruct(index.shape + values.shape[1:], dtype),
        in_specs=[pl.BlockSpec(memory_space=pltpu.SMEM)] * 2
        + [pl.BlockSpec(memory_space=pltpu.VMEM)],
        out_specs=pl.BlockSpec(memory_space=pltpu.VMEM),
        compiler_params=pltpu.CompilerParams(vmem_limit_bytes=48 * 2**20),
    )(index.astype(jnp.int32), keep.astype(jnp.int32), values)


MESH = pl.DeviceIdType.MESH


def part_of(ref, dim, at, size):
    index = [slice(None)] * len(ref.shape)
    index[dim] = pl.ds(at * size, size)
    return ref.at[tuple(index)]


def exchange_kernel(jobs, axes, *refs):
    count = len(jobs)
    sources, outs, sems = refs[:count], refs[count : 2 * count], refs[2 * count :]
    barrier = pltpu.get_barrier_semaphore()
    greeted = 0
    for axis, size in axes:
        me = lax.axis_index(axis)
        for step in range(1, size):
            pl.semaphore_signal(
                barrier, inc=1, device_id={axis: lax.rem(me + step, size)}, device_id_type=MESH
            )
            greeted += 1
    pl.semaphore_wait(barrier, greeted)
    started, relays, arrivals = [], [], []

    def remote(job_at, number, source, target, axis, device):
        return pltpu.make_async_remote_copy(
            src_ref=source,
            dst_ref=target,
            send_sem=sems[job_at].at[0, number],
            recv_sem=sems[job_at].at[1, number],
            device_id={axis: device},
            device_id_type=MESH,
        )

    sizes = dict(axes)
    for job_at, (kind, axis, dim, relay) in enumerate(jobs):
        size = sizes[axis]
        me = lax.axis_index(axis)
        source, out = sources[job_at], outs[job_at]
        if kind == "scatter":
            width = source.shape[dim] // size
            for step in range(1, size):
                other, origin = lax.rem(me + step, size), lax.rem(me + size - step, size)
                copy = remote(
                    job_at, step, part_of(source, dim, other, width), out.at[me], axis, other
                )
                copy.start()
                started.append(copy)
                arrivals.append(
                    remote(job_at, step, part_of(source, dim, me, width), out.at[origin], axis, other)
                )
            local = pltpu.make_async_copy(
                part_of(source, dim, me, width), out.at[me], sems[job_at].at[0, 0]
            )
        else:
            width = source.shape[dim]
            mine = part_of(out, dim, me, width)
            if relay:
                chips = size // 2
                chip, core = me // 2, lax.rem(me, 2)
                sibling = chip * 2 + 1 - core
                for step in range(1, chips):
                    other = lax.rem(chip + step, chips) * 2 + core
                    copy = remote(job_at, step, source, mine, axis, other)
                    copy.start()
                    started.append(copy)
                copy = remote(job_at, chips, source, mine, axis, sibling)
                copy.start()
                started.append(copy)
                arrivals.append(
                    remote(job_at, chips, source, part_of(out, dim, sibling, width), axis, sibling)
                )
                for step in range(1, chips):
                    origin = lax.rem(chip + chips - step, chips) * 2
                    here = part_of(out, dim, origin + core, width)
                    there = part_of(out, dim, origin + 1 - core, width)
                    relays.append(
                        (
                            remote(job_at, step, source, here, axis, sibling),
                            remote(job_at, chips + step, here, here, axis, sibling),
                        )
                    )
                    arrivals.append(remote(job_at, chips + step, source, there, axis, sibling))
            else:
                for step in range(1, size):
                    other, origin = lax.rem(me + step, size), lax.rem(me + size - step, size)
                    copy = remote(job_at, step, source, mine, axis, other)
                    copy.start()
                    started.append(copy)
                    arrivals.append(
                        remote(job_at, step, source, part_of(out, dim, origin, width), axis, other)
                    )
            local = pltpu.make_async_copy(source, mine, sems[job_at].at[0, 0])
        local.start()
        relays.append((local, None))
    for first, onward in relays:
        if onward is None:
            first.wait()
        else:
            first.wait_recv()
            onward.start()
            started.append(onward)
    for copy in arrivals:
        copy.wait_recv()
    for copy in started:
        copy.wait_send()


def exchange(mesh_shape, collective_id, *tasks):
    used = [axis for axis in ("dp", "tensor") if any(task[2] == axis for task in tasks)]
    axes = tuple((axis, mesh_shape[axis]) for axis in used)
    shapes, sems = [], []
    for values, kind, axis, dim, relay in tasks:
        size = mesh_shape[axis]
        shape = list(values.shape)
        if kind == "scatter":
            shape[dim] //= size
            shape = [size] + shape
        else:
            shape[dim] *= size
        shapes.append(jax.ShapeDtypeStruct(tuple(shape), values.dtype))
        sems.append(pltpu.SemaphoreType.DMA((2, size + 1)))
    sent = sum(values.size * values.dtype.itemsize for values, *_ in tasks)
    return pl.pallas_call(
        functools.partial(exchange_kernel, tuple(task[1:] for task in tasks), axes),
        out_shape=shapes,
        in_specs=[pl.BlockSpec(memory_space=pl.ANY)] * len(tasks),
        out_specs=[pl.BlockSpec(memory_space=pl.ANY)] * len(tasks),
        scratch_shapes=sems,
        cost_estimate=pl.CostEstimate(flops=0, bytes_accessed=8 * sent, transcendentals=0),
        compiler_params=pltpu.CompilerParams(collective_id=collective_id, has_side_effects=True),
    )(*(task[0] for task in tasks))


def rms_scale(values, gain_row):
    meansq = jnp.mean(values * values, axis=-1, keepdims=True)
    return (values * lax.rsqrt(meansq + 1e-05) * gain_row).astype(jnp.bfloat16)


def update_state(past_block, key_rows, value_rows, head_decay):
    event_count = key_rows.shape[2]
    position = jnp.arange(event_count).astype(jnp.float32)
    key_scale = key_rows.shape[3] ** (-0.5)
    factor = jnp.exp(-head_decay[:, None] * (event_count - 1.0 - position)[None, :])
    weighted = key_rows.astype(jnp.float32) * key_scale * factor[:, :, None]
    carried = jnp.exp(-head_decay * event_count)[:, None, None] * past_block
    return carried + jnp.einsum(
        "ghjd,ghje->ghde", weighted.astype(jnp.bfloat16), value_rows, preferred_element_type=jnp.float32
    )


def retain_events(query, key_rows, value_rows, past_block, head_decay):
    event_count = query.shape[2]
    position = jnp.arange(event_count).astype(jnp.float32)
    distance = position[:, None] - position[None, :]
    decay = jnp.where(
        distance >= 0, jnp.exp(-head_decay[:, None, None] * jnp.maximum(distance, 0.0)), 0.0
    )
    key_scale = query.shape[3] ** (-0.5)
    scores = (
        jnp.einsum("ghid,ghjd->ghij", query, key_rows, preferred_element_type=jnp.float32)
        * key_scale
    )
    weights_mix = (scores * decay).astype(jnp.bfloat16)
    intra_term = jnp.einsum(
        "ghij,ghje->ghie", weights_mix, value_rows, preferred_element_type=jnp.float32
    )
    inter_factor = jnp.exp(-head_decay[:, None] * (position[None, :] + 1.0))[:, :, None]
    inter_term = (
        jnp.einsum(
            "ghid,ghde->ghie",
            query,
            past_block.astype(jnp.bfloat16),
            preferred_element_type=jnp.float32,
        )
        * inter_factor
    )
    return intra_term + inter_term


def per_device(
    mesh_shape, tokens, past_states, attn_weights, ffn_weights, norm_gains, head_rates, end_lengths, new_slot
):
    sessions_here = end_lengths.shape[0]
    row_count = tokens.shape[0]
    event_count = row_count // sessions_here
    heads_here = past_states.shape[1]
    head_dim = past_states.shape[3]
    tensor_at = lax.axis_index("tensor")
    head_decay = lax.dynamic_slice_in_dim(head_rates, tensor_at * heads_here, heads_here)
    peer_count = lax.axis_size("dp")
    pair_cap = max(2, 2 * sessions_here // peer_count)
    slot_count = peer_count * pair_cap
    survive = end_lengths > event_count
    live_len = jnp.minimum(end_lengths, event_count)
    target_dev = new_slot // sessions_here
    local_slot = new_slot % sessions_here
    session_ids = jnp.arange(sessions_here, dtype=jnp.int32)
    earlier = (
        (target_dev[None, :] == target_dev[:, None])
        & survive[None, :]
        & (session_ids[None, :] < session_ids[:, None])
    )
    pair_rank = jnp.sum(earlier, axis=1)
    buffer_pos = target_dev * pair_cap + pair_rank
    matches = (buffer_pos[None, :] == jnp.arange(slot_count, dtype=jnp.int32)[:, None]) & survive[
        None, :
    ]
    source = jnp.sum(jnp.where(matches, session_ids[None, :], 0), axis=1)
    filled = jnp.any(matches, axis=1)
    label_at = jnp.sum(jnp.where(matches, local_slot[None, :], 0), axis=1)
    labels = jnp.where(filled, label_at, -1).reshape(peer_count, 1, pair_cap)
    labels = jnp.pad(labels, ((0, 0), (0, 7), (0, 128 - pair_cap)), constant_values=-1)
    weights_attn, weights_out, sent_labels = exchange(
        mesh_shape,
        0,
        (attn_weights[:4], "gather", "dp", 1, True),
        (attn_weights[4], "gather", "tensor", 1, False),
        (labels.astype(jnp.int32), "scatter", "dp", 0, False),
    )
    sent_labels = sent_labels[:, 0, 0, :pair_cap]
    float_tokens = tokens.astype(jnp.float32)
    normed = rms_scale(float_tokens, norm_gains[0])
    projected = jnp.einsum(
        "nd,mde->mne", normed, weights_attn, preferred_element_type=jnp.float32
    )

    def split_heads(matrix):
        return matrix.reshape(sessions_here, event_count, heads_here, head_dim).transpose(
            0, 2, 1, 3
        )

    query = split_heads(projected[0].astype(jnp.bfloat16))
    key_rows = split_heads(projected[1].astype(jnp.bfloat16))
    value_rows = split_heads(projected[2].astype(jnp.bfloat16))
    gate_rows = projected[3]
    retained = retain_events(query, key_rows, value_rows, past_states, head_decay)
    updated = update_state(past_states, key_rows, value_rows, head_decay)
    packed = pick(updated, source, filled, jnp.bfloat16)
    row_mean = jnp.mean(retained, axis=-1, keepdims=True)
    centred = retained - row_mean
    row_var = jnp.mean(centred * centred, axis=-1, keepdims=True)
    normalised = centred * lax.rsqrt(row_var + 1e-05)
    merged = normalised.transpose(0, 2, 1, 3).reshape(row_count, heads_here * head_dim)
    gated = (jax.nn.silu(gate_rows) * merged).astype(jnp.bfloat16)
    gated_all, weights_out, weights_ffn = exchange(
        mesh_shape,
        1,
        (gated, "gather", "tensor", 1, False),
        (weights_out, "gather", "dp", 0, True),
        (ffn_weights, "gather", "dp", 1, True),
    )
    attended = jnp.einsum("nc,dc->nd", gated_all, weights_out, preferred_element_type=jnp.float32)
    residual = float_tokens + attended
    hidden_in = rms_scale(residual, norm_gains[1])
    activated = jax.nn.gelu(
        jnp.dot(hidden_in, weights_ffn[0], preferred_element_type=jnp.float32), approximate=True
    ).astype(jnp.bfloat16)
    ffn_partial = jnp.einsum(
        "nf,df->nd", activated, weights_ffn[1], preferred_element_type=jnp.float32
    )
    ffn_terms, received = exchange(
        mesh_shape,
        2,
        (ffn_partial.astype(jnp.bfloat16), "scatter", "tensor", 1, False),
        (packed, "scatter", "dp", 0, False),
    )
    ffn_share = jnp.sum(ffn_terms.astype(jnp.float32), axis=0)
    flattened = received.reshape(packed.shape)
    found_at = sent_labels.reshape(-1)[None, :] == session_ids[:, None]
    which_slot = jnp.sum(
        jnp.where(found_at, jnp.arange(slot_count, dtype=jnp.int32)[None, :], 0), axis=1
    )
    present = jnp.any(found_at, axis=1)
    moved_states = pick(flattened, which_slot, present, jnp.float32)
    col_count = ffn_share.shape[1]
    residual_here = lax.dynamic_slice_in_dim(residual, tensor_at * col_count, col_count, 1)
    keep_rows = (jnp.arange(event_count, dtype=jnp.int32)[None, :] < live_len[:, None]).reshape(-1)
    next_tokens = jnp.where(keep_rows[:, None], residual_here + ffn_share, 0.0).astype(jnp.bfloat16)
    return (next_tokens, moved_states)


def solution(mesh):
    placed = (
        P(("group", "dp"), None),
        P(("group", "dp"), "tensor", None, None),
        P(None, "dp", "tensor"),
        P(None, "dp", "tensor"),
        P(),
        P(),
        P(("group", "dp")),
        P(("group", "dp")),
    )
    return jax.shard_map(
        functools.partial(per_device, dict(mesh.shape)),
        mesh=mesh,
        in_specs=placed,
        out_specs=(P(("group", "dp"), "tensor"), P(("group", "dp"), "tensor", None, None)),
        check_vma=False,
    )
```

```python
import functools

import jax
import jax.numpy as jnp
from jax import lax
from jax.experimental import pallas as pl
from jax.experimental.pallas import tpu as pltpu
from jax.sharding import PartitionSpec as P


def pick_kernel(index_ref, keep_ref, values_ref, out_ref):
    def body(at, carry):
        kept = keep_ref[at].astype(jnp.float32)
        out_ref[at] = jnp.where(
            kept > 0, values_ref[index_ref[at]].astype(jnp.float32), 0.0
        ).astype(out_ref.dtype)
        return carry

    lax.fori_loop(0, out_ref.shape[0], body, 0)


def pick(values, index, keep, dtype):
    return pl.pallas_call(
        pick_kernel,
        out_shape=jax.ShapeDtypeStruct(index.shape + values.shape[1:], dtype),
        in_specs=[pl.BlockSpec(memory_space=pltpu.SMEM)] * 2
        + [pl.BlockSpec(memory_space=pltpu.VMEM)],
        out_specs=pl.BlockSpec(memory_space=pltpu.VMEM),
        compiler_params=pltpu.CompilerParams(vmem_limit_bytes=48 * 2**20),
    )(index.astype(jnp.int32), keep.astype(jnp.int32), values)


MESH = pl.DeviceIdType.MESH


def part_of(ref, dim, at, size):
    index = [slice(None)] * len(ref.shape)
    index[dim] = pl.ds(at * size, size)
    return ref.at[tuple(index)]


def exchange_kernel(jobs, axes, *refs):
    count = len(jobs)
    sources, outs = refs[:count], refs[count : 2 * count]
    sems, held = refs[2 * count : 3 * count], refs[3 * count :]
    barrier = pltpu.get_barrier_semaphore()
    greeted = 0
    for axis, size in axes:
        me = lax.axis_index(axis)
        for step in range(1, size):
            pl.semaphore_signal(
                barrier, inc=1, device_id={axis: lax.rem(me + step, size)}, device_id_type=MESH
            )
            greeted += 1
    pl.semaphore_wait(barrier, greeted)
    sizes = dict(axes)
    events, arrivals, started, locals_ = [], [], [], []

    def remote(job_at, number, source, target, axis, device):
        return pltpu.make_async_remote_copy(
            src_ref=source,
            dst_ref=target,
            send_sem=sems[job_at].at[0, number],
            recv_sem=sems[job_at].at[1, number],
            device_id={axis: device},
            device_id_type=MESH,
        )

    def begin(copy):
        copy.start()
        started.append(copy.wait_send)

    def plain(job_at, source, out, axis, dim, kind):
        size = sizes[axis]
        me = lax.axis_index(axis)
        width = source.shape[dim] // (size if kind == "scatter" else 1)
        for step in range(1, size):
            other, origin = lax.rem(me + step, size), lax.rem(me + size - step, size)
            if kind == "scatter":
                block, put = part_of(source, dim, other, width), out.at[me]
                got = out.at[origin]
            else:
                block, put = source, part_of(out, dim, me, width)
                got = part_of(out, dim, origin, width)
            begin(remote(job_at, step, block, put, axis, other))
            arrivals.append(remote(job_at, step, block, got, axis, other).wait_recv)

    def relay(job_at, source, out, axis, dim):
        size, groups = sizes[axis], sizes["group"]
        me, group = lax.axis_index(axis), lax.axis_index("group")
        chips, chip, core = size // 2, me // 2, lax.rem(me, 2)
        sibling = chip * 2 + 1 - core
        width = source.shape[dim]
        turns = relay_turns(width, groups)
        chunk = width // (turns * groups)

        def place(ref, owner, at):
            return part_of(ref, dim, owner * (turns * groups) + at, chunk)

        number = iter(range(1, 1 << 16))
        for turn in range(turns):
            at = turn * groups + group
            for step in range(1, chips):
                other = lax.rem(chip + step, chips) * 2 + core
                origin = lax.rem(chip + chips - step, chips) * 2
                over, down = next(number), next(number)
                begin(remote(job_at, over, place(source, 0, at), place(out, me, at), axis, other))
                here, there = place(out, origin + core, at), place(out, origin + 1 - core, at)
                ways = [next(number) for _ in range(2 * (groups - 1))]

                def arrive(over=over, down=down, here=here, ways=ways):
                    remote(job_at, over, here, here, axis, sibling).wait_recv()
                    for shift in range(1, groups):
                        begin(
                            remote(
                                job_at, ways[shift - 1], here, here, "group",
                                lax.rem(group + shift, groups),
                            )
                        )
                    begin(remote(job_at, down, here, here, axis, sibling))

                events.append(((turn + 1) / turns, arrive))
                arrivals.append(remote(job_at, down, there, there, axis, sibling).wait_recv)
                for shift in range(1, groups):
                    late = turn * groups + lax.rem(group + groups - shift, groups)
                    first, last = ways[shift - 1], ways[groups - 2 + shift]
                    here, there = place(out, origin + core, late), place(out, origin + 1 - core, late)

                    def hand(first=first, last=last, here=here):
                        remote(job_at, first, here, here, axis, sibling).wait_recv()
                        begin(remote(job_at, last, here, here, axis, sibling))

                    events.append(((turn + 2.1) / turns, hand))
                    arrivals.append(remote(job_at, last, there, there, axis, sibling).wait_recv)
        whole = next(number)
        begin(remote(job_at, whole, source, part_of(out, dim, me, width), axis, sibling))
        got = part_of(out, dim, sibling, width)
        arrivals.append(remote(job_at, whole, source, got, axis, sibling).wait_recv)

    def chain(job_at, source, out, axis, dim):
        size = sizes[axis]
        me = lax.axis_index(axis)
        width, rows = source.shape[dim], source.shape[0]
        cuts = CHAIN_CUTS
        for step in range(size):
            for cut in range(cuts):
                across = pl.ds(cut * (rows // cuts), rows // cuts)
                for way, sign in enumerate((1, -1)):
                    origin = me - sign * step
                    held = (origin >= 0) & (origin < size)
                    onward = held & (me + sign >= 0) & (me + sign < size)
                    safe = jnp.clip(origin, 0, size - 1)
                    there = out.at[across, pl.ds(safe * width, width)]
                    block = source.at[across] if step == 0 else there
                    now = 1 + (step * cuts + cut) * 2 + way
                    after = now + 2 * cuts
                    neighbour = jnp.clip(me + sign, 0, size - 1)

                    def act(step=step, now=now, after=after, there=there, block=block, held=held,
                            onward=onward, neighbour=neighbour):
                        if step > 0:
                            pl.when(held)(
                                lambda: remote(job_at, now, there, there, axis, neighbour).wait_recv()
                            )
                        if step < size - 1:
                            copy = remote(job_at, after, block, there, axis, neighbour)
                            pl.when(onward)(lambda: copy.start())
                            started.append(lambda: pl.when(onward)(lambda: copy.wait_send()))

                    if step == 0:
                        act()
                    else:
                        events.append(((step - 1 + (cut + 1) / cuts) / (size - 1), act))

    for job_at, (kind, axis, dim, lead) in enumerate(jobs):
        source, out = sources[job_at], outs[job_at]
        if lead:
            source = source.at[lead[0] : lead[1]] if lead[1] > lead[0] + 1 else source.at[lead[0]]
        me = lax.axis_index(axis)
        if kind == "relay":
            relay(job_at, source, out, axis, dim)
        elif kind == "chain":
            chain(job_at, source, out, axis, dim)
        else:
            plain(job_at, source, out, axis, dim, kind)
        if kind == "scatter":
            block = part_of(source, dim, me, source.shape[dim] // sizes[axis])
            mine = out.at[me]
        else:
            block, mine = source, part_of(out, dim, me, source.shape[dim])
        locals_.append(
            (
                pltpu.make_async_copy(block, held[job_at], sems[job_at].at[0, 0]),
                pltpu.make_async_copy(held[job_at], mine, sems[job_at].at[1, 0]),
            )
        )
    for fetch, _ in locals_:
        fetch.start()
    for fetch, put in locals_:
        fetch.wait()
        put.start()
        arrivals.append(put.wait)
    for _, act in sorted(events, key=lambda event: event[0]):
        act()
    for wait in arrivals:
        wait()
    for wait in started:
        wait()


CHAIN_CUTS = 4


def relay_turns(width, groups):
    return max(1, min(8, width // 16) // groups)


def exchange(mesh_shape, collective_id, *tasks):
    used = [task[2] for task in tasks] + ["group" for task in tasks if task[1] == "relay"]
    axes = tuple((axis, mesh_shape[axis]) for axis in ("group", "dp", "tensor") if axis in used)
    shapes, sems, held = [], [], []
    for values, kind, axis, dim, lead in tasks:
        size = mesh_shape[axis]
        shape = list(values.shape)
        if lead:
            shape = ([lead[1] - lead[0]] if lead[1] > lead[0] + 1 else []) + shape[1:]
        number = size + 1
        if kind == "relay":
            groups = mesh_shape["group"]
            turns = relay_turns(shape[dim], groups)
            number = 2 + turns * (size // 2 - 1) * 2 * groups
        elif kind == "chain":
            number = 1 + 2 * CHAIN_CUTS * size
        if kind == "scatter":
            shape[dim] //= size
            held.append(pltpu.VMEM(tuple(shape), values.dtype))
            shape = [size] + shape
        else:
            held.append(pltpu.VMEM(tuple(shape), values.dtype))
            shape[dim] *= size
        shapes.append(jax.ShapeDtypeStruct(tuple(shape), values.dtype))
        sems.append(pltpu.SemaphoreType.DMA((2, number)))
    sent = sum(values.size * values.dtype.itemsize for values, *_ in tasks)
    return pl.pallas_call(
        functools.partial(exchange_kernel, tuple(task[1:] for task in tasks), axes),
        out_shape=shapes,
        in_specs=[pl.BlockSpec(memory_space=pl.ANY)] * len(tasks),
        out_specs=[pl.BlockSpec(memory_space=pl.ANY)] * len(tasks),
        scratch_shapes=sems + held,
        cost_estimate=pl.CostEstimate(flops=0, bytes_accessed=8 * sent, transcendentals=0),
        compiler_params=pltpu.CompilerParams(
            collective_id=collective_id, has_side_effects=True, vmem_limit_bytes=16 * 2**20
        ),
    )(*(task[0] for task in tasks))


def rms_scale(values, gain_row):
    meansq = jnp.mean(values * values, axis=-1, keepdims=True)
    return (values * lax.rsqrt(meansq + 1e-05) * gain_row).astype(jnp.bfloat16)


def update_state(past_block, key_rows, value_rows, head_decay):
    event_count = key_rows.shape[2]
    position = jnp.arange(event_count).astype(jnp.float32)
    key_scale = key_rows.shape[3] ** (-0.5)
    factor = jnp.exp(-head_decay[:, None] * (event_count - 1.0 - position)[None, :])
    weighted = key_rows.astype(jnp.float32) * key_scale * factor[:, :, None]
    carried = jnp.exp(-head_decay * event_count)[:, None, None] * past_block
    return carried + jnp.einsum(
        "ghjd,ghje->ghde", weighted.astype(jnp.bfloat16), value_rows, preferred_element_type=jnp.float32
    )


def retain_events(query, key_rows, value_rows, past_block, head_decay):
    event_count = query.shape[2]
    position = jnp.arange(event_count).astype(jnp.float32)
    distance = position[:, None] - position[None, :]
    decay = jnp.where(
        distance >= 0, jnp.exp(-head_decay[:, None, None] * jnp.maximum(distance, 0.0)), 0.0
    )
    key_scale = query.shape[3] ** (-0.5)
    scores = (
        jnp.einsum("ghid,ghjd->ghij", query, key_rows, preferred_element_type=jnp.float32)
        * key_scale
    )
    weights_mix = (scores * decay).astype(jnp.bfloat16)
    intra_term = jnp.einsum(
        "ghij,ghje->ghie", weights_mix, value_rows, preferred_element_type=jnp.float32
    )
    inter_factor = jnp.exp(-head_decay[:, None] * (position[None, :] + 1.0))[:, :, None]
    inter_term = (
        jnp.einsum(
            "ghid,ghde->ghie",
            query,
            past_block.astype(jnp.bfloat16),
            preferred_element_type=jnp.float32,
        )
        * inter_factor
    )
    return intra_term + inter_term


def per_device(
    mesh_shape, tokens, past_states, attn_weights, ffn_weights, norm_gains, head_rates, end_lengths, new_slot
):
    sessions_here = end_lengths.shape[0]
    row_count = tokens.shape[0]
    event_count = row_count // sessions_here
    heads_here = past_states.shape[1]
    head_dim = past_states.shape[3]
    tensor_at = lax.axis_index("tensor")
    head_decay = lax.dynamic_slice_in_dim(head_rates, tensor_at * heads_here, heads_here)
    peer_count = lax.axis_size("dp")
    pair_cap = max(2, 2 * sessions_here // peer_count)
    slot_count = peer_count * pair_cap
    survive = end_lengths > event_count
    live_len = jnp.minimum(end_lengths, event_count)
    target_dev = new_slot // sessions_here
    local_slot = new_slot % sessions_here
    session_ids = jnp.arange(sessions_here, dtype=jnp.int32)
    earlier = (
        (target_dev[None, :] == target_dev[:, None])
        & survive[None, :]
        & (session_ids[None, :] < session_ids[:, None])
    )
    pair_rank = jnp.sum(earlier, axis=1)
    buffer_pos = target_dev * pair_cap + pair_rank
    matches = (buffer_pos[None, :] == jnp.arange(slot_count, dtype=jnp.int32)[:, None]) & survive[
        None, :
    ]
    source = jnp.sum(jnp.where(matches, session_ids[None, :], 0), axis=1)
    filled = jnp.any(matches, axis=1)
    label_at = jnp.sum(jnp.where(matches, local_slot[None, :], 0), axis=1)
    labels = jnp.where(filled, label_at, -1).reshape(peer_count, 1, pair_cap)
    labels = jnp.pad(labels, ((0, 0), (0, 7), (0, 128 - pair_cap)), constant_values=-1)
    weights_attn, weights_out, sent_labels = exchange(
        mesh_shape,
        0,
        (attn_weights, "relay", "dp", 1, (0, 4)),
        (attn_weights, "gather", "tensor", 1, (4, 5)),
        (labels.astype(jnp.int32), "scatter", "dp", 0, None),
    )
    sent_labels = sent_labels[:, 0, 0, :pair_cap]
    float_tokens = tokens.astype(jnp.float32)
    normed = rms_scale(float_tokens, norm_gains[0])
    projected = jnp.einsum(
        "nd,mde->mne", normed, weights_attn, preferred_element_type=jnp.float32
    )

    def split_heads(matrix):
        return matrix.reshape(sessions_here, event_count, heads_here, head_dim).transpose(
            0, 2, 1, 3
        )

    query = split_heads(projected[0].astype(jnp.bfloat16))
    key_rows = split_heads(projected[1].astype(jnp.bfloat16))
    value_rows = split_heads(projected[2].astype(jnp.bfloat16))
    gate_rows = projected[3]
    retained = retain_events(query, key_rows, value_rows, past_states, head_decay)
    updated = update_state(past_states, key_rows, value_rows, head_decay)
    packed = pick(updated, source, filled, jnp.bfloat16)
    row_mean = jnp.mean(retained, axis=-1, keepdims=True)
    centred = retained - row_mean
    row_var = jnp.mean(centred * centred, axis=-1, keepdims=True)
    normalised = centred * lax.rsqrt(row_var + 1e-05)
    merged = normalised.transpose(0, 2, 1, 3).reshape(row_count, heads_here * head_dim)
    gated = (jax.nn.silu(gate_rows) * merged).astype(jnp.bfloat16)
    gated_all, weights_out, weights_ffn = exchange(
        mesh_shape,
        1,
        (gated, "chain", "tensor", 1, None),
        (weights_out, "relay", "dp", 0, None),
        (ffn_weights, "relay", "dp", 1, None),
    )
    attended = jnp.einsum("nc,dc->nd", gated_all, weights_out, preferred_element_type=jnp.float32)
    residual = float_tokens + attended
    hidden_in = rms_scale(residual, norm_gains[1])
    activated = jax.nn.gelu(
        jnp.dot(hidden_in, weights_ffn[0], preferred_element_type=jnp.float32), approximate=True
    ).astype(jnp.bfloat16)
    ffn_partial = jnp.einsum(
        "nf,df->nd", activated, weights_ffn[1], preferred_element_type=jnp.float32
    )
    ffn_terms, received = exchange(
        mesh_shape,
        2,
        (ffn_partial.astype(jnp.bfloat16), "scatter", "tensor", 1, None),
        (packed, "scatter", "dp", 0, None),
    )
    ffn_share = jnp.sum(ffn_terms.astype(jnp.float32), axis=0)
    flattened = received.reshape(packed.shape)
    found_at = sent_labels.reshape(-1)[None, :] == session_ids[:, None]
    which_slot = jnp.sum(
        jnp.where(found_at, jnp.arange(slot_count, dtype=jnp.int32)[None, :], 0), axis=1
    )
    present = jnp.any(found_at, axis=1)
    moved_states = pick(flattened, which_slot, present, jnp.float32)
    col_count = ffn_share.shape[1]
    residual_here = lax.dynamic_slice_in_dim(residual, tensor_at * col_count, col_count, 1)
    keep_rows = (jnp.arange(event_count, dtype=jnp.int32)[None, :] < live_len[:, None]).reshape(-1)
    next_tokens = jnp.where(keep_rows[:, None], residual_here + ffn_share, 0.0).astype(jnp.bfloat16)
    return (next_tokens, moved_states)


def solution(mesh):
    placed = (
        P(("group", "dp"), None),
        P(("group", "dp"), "tensor", None, None),
        P(None, "dp", "tensor"),
        P(None, "dp", "tensor"),
        P(),
        P(),
        P(("group", "dp")),
        P(("group", "dp")),
    )
    return jax.shard_map(
        functools.partial(per_device, dict(mesh.shape)),
        mesh=mesh,
        in_specs=placed,
        out_specs=(P(("group", "dp"), "tensor"), P(("group", "dp"), "tensor", None, None)),
        check_vma=False,
    )
```

```python
import functools

import jax
import jax.numpy as jnp
from jax import lax
from jax.experimental import pallas as pl
from jax.experimental.pallas import tpu as pltpu
from jax.sharding import PartitionSpec as P


def pick_kernel(index_ref, keep_ref, values_ref, out_ref):
    def body(at, carry):
        kept = keep_ref[at].astype(jnp.float32)
        out_ref[at] = jnp.where(
            kept > 0, values_ref[index_ref[at]].astype(jnp.float32), 0.0
        ).astype(out_ref.dtype)
        return carry

    lax.fori_loop(0, out_ref.shape[0], body, 0)


def pick(values, index, keep, dtype):
    return pl.pallas_call(
        pick_kernel,
        out_shape=jax.ShapeDtypeStruct(index.shape + values.shape[1:], dtype),
        in_specs=[pl.BlockSpec(memory_space=pltpu.SMEM)] * 2
        + [pl.BlockSpec(memory_space=pltpu.VMEM)],
        out_specs=pl.BlockSpec(memory_space=pltpu.VMEM),
        compiler_params=pltpu.CompilerParams(vmem_limit_bytes=48 * 2**20),
    )(index.astype(jnp.int32), keep.astype(jnp.int32), values)


MESH = pl.DeviceIdType.MESH


def part_of(ref, dim, at, size):
    index = [slice(None)] * len(ref.shape)
    index[dim] = pl.ds(at * size, size)
    return ref.at[tuple(index)]


def exchange_kernel(jobs, axes, with_norm, *refs):
    count = len(jobs)
    if with_norm:
        (rows_ref, gain_ref), normed_ref = refs[count : count + 2], refs[2 * count + 2]
        refs = refs[:count] + refs[count + 2 : 2 * count + 2] + refs[2 * count + 3 :]
    sources, outs = refs[:count], refs[count : 2 * count]
    sems, held = refs[2 * count : 3 * count], refs[3 * count :]
    barrier = pltpu.get_barrier_semaphore()
    greeted = 0
    for axis, size in axes:
        me = lax.axis_index(axis)
        for step in range(1, size):
            pl.semaphore_signal(
                barrier, inc=1, device_id={axis: lax.rem(me + step, size)}, device_id_type=MESH
            )
            greeted += 1
    pl.semaphore_wait(barrier, greeted)
    sizes = dict(axes)
    events, arrivals, started, locals_ = [], [], [], []

    def remote(job_at, number, source, target, axis, device):
        return pltpu.make_async_remote_copy(
            src_ref=source,
            dst_ref=target,
            send_sem=sems[job_at].at[0, number],
            recv_sem=sems[job_at].at[1, number],
            device_id={axis: device},
            device_id_type=MESH,
        )

    def begin(copy):
        copy.start()
        started.append(copy.wait_send)

    def plain(job_at, source, out, axis, dim, kind):
        size = sizes[axis]
        me = lax.axis_index(axis)
        width = source.shape[dim] // (size if kind == "scatter" else 1)
        for step in range(1, size):
            other, origin = lax.rem(me + step, size), lax.rem(me + size - step, size)
            if kind == "scatter":
                block, put = part_of(source, dim, other, width), out.at[me]
                got = out.at[origin]
            else:
                block, put = source, part_of(out, dim, me, width)
                got = part_of(out, dim, origin, width)
            begin(remote(job_at, step, block, put, axis, other))
            arrivals.append(remote(job_at, step, block, got, axis, other).wait_recv)

    def relay(job_at, source, out, axis, dim):
        size, groups = sizes[axis], sizes["group"]
        me, group = lax.axis_index(axis), lax.axis_index("group")
        chips, chip, core = size // 2, me // 2, lax.rem(me, 2)
        sibling = chip * 2 + 1 - core
        width = source.shape[dim]
        turns = relay_turns(width, groups)
        chunk = width // (turns * groups)

        def place(ref, owner, at):
            return part_of(ref, dim, owner * (turns * groups) + at, chunk)

        number = iter(range(1, 1 << 16))
        for turn in range(turns):
            at = turn * groups + group
            for step in range(1, chips):
                other = lax.rem(chip + step, chips) * 2 + core
                origin = lax.rem(chip + chips - step, chips) * 2
                over, down = next(number), next(number)
                begin(remote(job_at, over, place(source, 0, at), place(out, me, at), axis, other))
                here, there = place(out, origin + core, at), place(out, origin + 1 - core, at)
                ways = [next(number) for _ in range(2 * (groups - 1))]

                def arrive(over=over, down=down, here=here, ways=ways):
                    remote(job_at, over, here, here, axis, sibling).wait_recv()
                    for shift in range(1, groups):
                        begin(
                            remote(
                                job_at, ways[shift - 1], here, here, "group",
                                lax.rem(group + shift, groups),
                            )
                        )
                    begin(remote(job_at, down, here, here, axis, sibling))

                events.append(((turn + 1) / turns, arrive))
                arrivals.append(remote(job_at, down, there, there, axis, sibling).wait_recv)
                for shift in range(1, groups):
                    late = turn * groups + lax.rem(group + groups - shift, groups)
                    first, last = ways[shift - 1], ways[groups - 2 + shift]
                    here, there = place(out, origin + core, late), place(out, origin + 1 - core, late)

                    def hand(first=first, last=last, here=here):
                        remote(job_at, first, here, here, axis, sibling).wait_recv()
                        begin(remote(job_at, last, here, here, axis, sibling))

                    events.append(((turn + 2.1) / turns, hand))
                    arrivals.append(remote(job_at, last, there, there, axis, sibling).wait_recv)
        whole = next(number)
        begin(remote(job_at, whole, source, part_of(out, dim, me, width), axis, sibling))
        got = part_of(out, dim, sibling, width)
        arrivals.append(remote(job_at, whole, source, got, axis, sibling).wait_recv)

    def chain(job_at, source, out, axis, dim):
        size = sizes[axis]
        me = lax.axis_index(axis)
        width, rows = source.shape[dim], source.shape[0]
        cuts = CHAIN_CUTS
        for step in range(size):
            for cut in range(cuts):
                across = pl.ds(cut * (rows // cuts), rows // cuts)
                for way, sign in enumerate((1, -1)):
                    origin = me - sign * step
                    held = (origin >= 0) & (origin < size)
                    onward = held & (me + sign >= 0) & (me + sign < size)
                    safe = jnp.clip(origin, 0, size - 1)
                    there = out.at[across, pl.ds(safe * width, width)]
                    block = source.at[across] if step == 0 else there
                    now = 1 + (step * cuts + cut) * 2 + way
                    after = now + 2 * cuts
                    neighbour = jnp.clip(me + sign, 0, size - 1)

                    def act(step=step, now=now, after=after, there=there, block=block, held=held,
                            onward=onward, neighbour=neighbour):
                        if step > 0:
                            pl.when(held)(
                                lambda: remote(job_at, now, there, there, axis, neighbour).wait_recv()
                            )
                        if step < size - 1:
                            copy = remote(job_at, after, block, there, axis, neighbour)
                            pl.when(onward)(lambda: copy.start())
                            started.append(lambda: pl.when(onward)(lambda: copy.wait_send()))

                    if step == 0:
                        act()
                    else:
                        events.append(((step - 1 + (cut + 1) / cuts) / (size - 1), act))

    for job_at, (kind, axis, dim, lead) in enumerate(jobs):
        source, out = sources[job_at], outs[job_at]
        if lead:
            source = source.at[lead[0] : lead[1]] if lead[1] > lead[0] + 1 else source.at[lead[0]]
        me = lax.axis_index(axis)
        if kind == "relay":
            relay(job_at, source, out, axis, dim)
        elif kind == "chain":
            chain(job_at, source, out, axis, dim)
        else:
            plain(job_at, source, out, axis, dim, kind)
        if kind == "scatter":
            block = part_of(source, dim, me, source.shape[dim] // sizes[axis])
            mine = out.at[me]
        else:
            block, mine = source, part_of(out, dim, me, source.shape[dim])
        locals_.append(
            (
                pltpu.make_async_copy(block, held[job_at], sems[job_at].at[0, 0]),
                pltpu.make_async_copy(held[job_at], mine, sems[job_at].at[1, 0]),
            )
        )
    for fetch, _ in locals_:
        fetch.start()
    for fetch, put in locals_:
        fetch.wait()
        put.start()
        arrivals.append(put.wait)
    if with_norm:
        step_rows = min(64, rows_ref.shape[0])

        def norm_step(at, carry):
            rows = pl.ds(pl.multiple_of(at * step_rows, step_rows), step_rows)
            normed_ref[rows] = rms_scale(rows_ref[rows].astype(jnp.float32), gain_ref[...])
            return carry

        lax.fori_loop(0, rows_ref.shape[0] // step_rows, norm_step, 0)
    for _, act in sorted(events, key=lambda event: event[0]):
        act()
    for wait in arrivals:
        wait()
    for wait in started:
        wait()


CHAIN_CUTS = 4


def relay_turns(width, groups):
    return max(1, min(8, width // 16) // groups)


def exchange(mesh_shape, collective_id, *tasks, norm=()):
    used = [task[2] for task in tasks] + ["group" for task in tasks if task[1] == "relay"]
    axes = tuple((axis, mesh_shape[axis]) for axis in ("group", "dp", "tensor") if axis in used)
    shapes, sems, held = [], [], []
    for values, kind, axis, dim, lead in tasks:
        size = mesh_shape[axis]
        shape = list(values.shape)
        if lead:
            shape = ([lead[1] - lead[0]] if lead[1] > lead[0] + 1 else []) + shape[1:]
        number = size + 1
        if kind == "relay":
            groups = mesh_shape["group"]
            turns = relay_turns(shape[dim], groups)
            number = 2 + turns * (size // 2 - 1) * 2 * groups
        elif kind == "chain":
            number = 1 + 2 * CHAIN_CUTS * size
        if kind == "scatter":
            shape[dim] //= size
            held.append(pltpu.VMEM(tuple(shape), values.dtype))
            shape = [size] + shape
        else:
            held.append(pltpu.VMEM(tuple(shape), values.dtype))
            shape[dim] *= size
        shapes.append(jax.ShapeDtypeStruct(tuple(shape), values.dtype))
        sems.append(pltpu.SemaphoreType.DMA((2, number)))
    in_vmem = [pl.BlockSpec(memory_space=pltpu.VMEM)]
    if norm:
        shapes.append(jax.ShapeDtypeStruct(norm[0].shape, jnp.bfloat16))
    sent = sum(values.size * values.dtype.itemsize for values, *_ in tasks)
    return pl.pallas_call(
        functools.partial(exchange_kernel, tuple(task[1:] for task in tasks), axes, bool(norm)),
        out_shape=shapes,
        in_specs=[pl.BlockSpec(memory_space=pl.ANY)] * len(tasks) + in_vmem * len(norm),
        out_specs=[pl.BlockSpec(memory_space=pl.ANY)] * len(tasks) + in_vmem * bool(norm),
        scratch_shapes=sems + held,
        cost_estimate=pl.CostEstimate(flops=0, bytes_accessed=8 * sent, transcendentals=0),
        compiler_params=pltpu.CompilerParams(
            collective_id=collective_id, has_side_effects=True, vmem_limit_bytes=16 * 2**20
        ),
    )(*(task[0] for task in tasks), *norm)


def rms_scale(values, gain_row):
    meansq = jnp.mean(values * values, axis=-1, keepdims=True)
    return (values * lax.rsqrt(meansq + 1e-05) * gain_row).astype(jnp.bfloat16)


def update_state(past_block, key_rows, value_rows, head_decay):
    event_count = key_rows.shape[2]
    position = jnp.arange(event_count).astype(jnp.float32)
    key_scale = key_rows.shape[3] ** (-0.5)
    factor = jnp.exp(-head_decay[:, None] * (event_count - 1.0 - position)[None, :])
    weighted = key_rows.astype(jnp.float32) * key_scale * factor[:, :, None]
    carried = jnp.exp(-head_decay * event_count)[:, None, None] * past_block
    return carried + jnp.einsum(
        "ghjd,ghje->ghde", weighted.astype(jnp.bfloat16), value_rows, preferred_element_type=jnp.float32
    )


def retain_events(query, key_rows, value_rows, past_block, head_decay):
    event_count = query.shape[2]
    position = jnp.arange(event_count).astype(jnp.float32)
    distance = position[:, None] - position[None, :]
    decay = jnp.where(
        distance >= 0, jnp.exp(-head_decay[:, None, None] * jnp.maximum(distance, 0.0)), 0.0
    )
    key_scale = query.shape[3] ** (-0.5)
    scores = (
        jnp.einsum("ghid,ghjd->ghij", query, key_rows, preferred_element_type=jnp.float32)
        * key_scale
    )
    weights_mix = (scores * decay).astype(jnp.bfloat16)
    intra_term = jnp.einsum(
        "ghij,ghje->ghie", weights_mix, value_rows, preferred_element_type=jnp.float32
    )
    inter_factor = jnp.exp(-head_decay[:, None] * (position[None, :] + 1.0))[:, :, None]
    inter_term = (
        jnp.einsum(
            "ghid,ghde->ghie",
            query,
            past_block.astype(jnp.bfloat16),
            preferred_element_type=jnp.float32,
        )
        * inter_factor
    )
    return intra_term + inter_term


def per_device(
    mesh_shape, tokens, past_states, attn_weights, ffn_weights, norm_gains, head_rates, end_lengths, new_slot
):
    sessions_here = end_lengths.shape[0]
    row_count = tokens.shape[0]
    event_count = row_count // sessions_here
    heads_here = past_states.shape[1]
    head_dim = past_states.shape[3]
    tensor_at = lax.axis_index("tensor")
    head_decay = lax.dynamic_slice_in_dim(head_rates, tensor_at * heads_here, heads_here)
    peer_count = lax.axis_size("dp")
    pair_cap = max(2, 2 * sessions_here // peer_count)
    slot_count = peer_count * pair_cap
    survive = end_lengths > event_count
    live_len = jnp.minimum(end_lengths, event_count)
    target_dev = new_slot // sessions_here
    local_slot = new_slot % sessions_here
    session_ids = jnp.arange(sessions_here, dtype=jnp.int32)
    earlier = (
        (target_dev[None, :] == target_dev[:, None])
        & survive[None, :]
        & (session_ids[None, :] < session_ids[:, None])
    )
    pair_rank = jnp.sum(earlier, axis=1)
    buffer_pos = target_dev * pair_cap + pair_rank
    matches = (buffer_pos[None, :] == jnp.arange(slot_count, dtype=jnp.int32)[:, None]) & survive[
        None, :
    ]
    source = jnp.sum(jnp.where(matches, session_ids[None, :], 0), axis=1)
    filled = jnp.any(matches, axis=1)
    label_at = jnp.sum(jnp.where(matches, local_slot[None, :], 0), axis=1)
    labels = jnp.where(filled, label_at, -1).reshape(peer_count, 1, pair_cap)
    labels = jnp.pad(labels, ((0, 0), (0, 7), (0, 128 - pair_cap)), constant_values=-1)
    weights_attn, weights_out, sent_labels, normed = exchange(
        mesh_shape,
        0,
        (attn_weights, "relay", "dp", 1, (0, 4)),
        (attn_weights, "gather", "tensor", 1, (4, 5)),
        (labels.astype(jnp.int32), "scatter", "dp", 0, None),
        norm=(tokens, norm_gains[:1]),
    )
    sent_labels = sent_labels[:, 0, 0, :pair_cap]
    float_tokens = tokens.astype(jnp.float32)
    projected = [
        jnp.dot(normed, weights_attn[which], preferred_element_type=jnp.float32)
        for which in range(4)
    ]

    def split_heads(matrix):
        return matrix.reshape(sessions_here, event_count, heads_here, head_dim).transpose(
            0, 2, 1, 3
        )

    query = split_heads(projected[0].astype(jnp.bfloat16))
    key_rows = split_heads(projected[1].astype(jnp.bfloat16))
    value_rows = split_heads(projected[2].astype(jnp.bfloat16))
    gate_rows = projected[3]
    retained = retain_events(query, key_rows, value_rows, past_states, head_decay)
    updated = update_state(past_states, key_rows, value_rows, head_decay)
    packed = pick(updated, source, filled, jnp.bfloat16)
    row_mean = jnp.mean(retained, axis=-1, keepdims=True)
    centred = retained - row_mean
    row_var = jnp.mean(centred * centred, axis=-1, keepdims=True)
    normalised = centred * lax.rsqrt(row_var + 1e-05)
    merged = normalised.transpose(0, 2, 1, 3).reshape(row_count, heads_here * head_dim)
    gated = (jax.nn.silu(gate_rows) * merged).astype(jnp.bfloat16)
    gated_all, weights_out, weights_ffn = exchange(
        mesh_shape,
        1,
        (gated, "chain", "tensor", 1, None),
        (weights_out, "relay", "dp", 0, None),
        (ffn_weights, "relay", "dp", 1, None),
    )
    attended = jnp.einsum("nc,dc->nd", gated_all, weights_out, preferred_element_type=jnp.float32)
    residual = float_tokens + attended
    hidden_in = rms_scale(residual, norm_gains[1])
    activated = jax.nn.gelu(
        jnp.dot(hidden_in, weights_ffn[0], preferred_element_type=jnp.float32), approximate=True
    ).astype(jnp.bfloat16)
    ffn_partial = jnp.einsum(
        "nf,df->nd", activated, weights_ffn[1], preferred_element_type=jnp.float32
    )
    ffn_terms, received = exchange(
        mesh_shape,
        2,
        (ffn_partial.astype(jnp.bfloat16), "scatter", "tensor", 1, None),
        (packed, "scatter", "dp", 0, None),
    )
    ffn_share = jnp.sum(ffn_terms.astype(jnp.float32), axis=0)
    flattened = received.reshape(packed.shape)
    found_at = sent_labels.reshape(-1)[None, :] == session_ids[:, None]
    which_slot = jnp.sum(
        jnp.where(found_at, jnp.arange(slot_count, dtype=jnp.int32)[None, :], 0), axis=1
    )
    present = jnp.any(found_at, axis=1)
    moved_states = pick(flattened, which_slot, present, jnp.float32)
    col_count = ffn_share.shape[1]
    residual_here = lax.dynamic_slice_in_dim(residual, tensor_at * col_count, col_count, 1)
    keep_rows = (jnp.arange(event_count, dtype=jnp.int32)[None, :] < live_len[:, None]).reshape(-1)
    next_tokens = jnp.where(keep_rows[:, None], residual_here + ffn_share, 0.0).astype(jnp.bfloat16)
    return (next_tokens, moved_states)


def solution(mesh):
    placed = (
        P(("group", "dp"), None),
        P(("group", "dp"), "tensor", None, None),
        P(None, "dp", "tensor"),
        P(None, "dp", "tensor"),
        P(),
        P(),
        P(("group", "dp")),
        P(("group", "dp")),
    )
    return jax.shard_map(
        functools.partial(per_device, dict(mesh.shape)),
        mesh=mesh,
        in_specs=placed,
        out_specs=(P(("group", "dp"), "tensor"), P(("group", "dp"), "tensor", None, None)),
        check_vma=False,
    )
```
